32 devices in a mesh: dom: 8 (over z, y), span: 4 (over x, core).
Axes of the slice: x: 2, y: 2, z: 4, core: 2. Of those that a mesh axis runs over, the one named last changes fastest.
Arguments:
- entities: bfloat16 [8192, 256], P('dom'), may hold values from -2.5 to 2.5
- operators: bfloat16 [64, 256, 256], P('span'), may hold values from -0.375 to 0.375
- left_rows: int32 [3, 8, 4, 512], P(None, 'dom', 'span'), may hold values from 0 to 1023
- right_rows: int32 [3, 8, 4, 512], P(None, 'dom', 'span'), may hold values from 0 to 1023
- negatives: int32 [3, 8, 4, 1024], P(None, 'dom', 'span'), may hold values from 0 to 1023
- counts: int32 [3, 8, 4, 64], P(None, 'dom', 'span'), may hold values from 1 to 8, as said below
Outputs:
- entity_grad: float32 [8192, 256], P(('dom', 'span'))
- relation_grad: float32 [64, 256, 256], P('span', 'dom')
The draws below stay inside these ranges and needn't reach their ends.
Inputs may be any that keep to these rules, and one draw needn't show every extreme that they name: `counts`: in every bucket step and partition one relation has all 8 slots live in every group's list.
All inputs are finite; a program needn't handle non-finite values.
Results may differ from the reference program's by a relative error of at most 0.0021.
Values may be sent and summed in bfloat16 or wider, within the bound.
A program may use at most 64 MiB of HBM per device.

```python
import jax
import jax.numpy as jnp
from jax import lax

D = 256
R = 64
NEG = 1024
CAP = 8
STEPS = 3
PART_ROWS = 1024
SLOTS = 512
ENT = 8192
N_DOM = 8
N_SPAN = 4


def draw_counts(key, part):
    key = jax.random.fold_in(key, 11)
    level_key, count_key, full_key = jax.random.split(key, 3)
    levels = jax.random.randint(level_key, (STEPS, N_DOM, N_SPAN, 1), CAP // 2, CAP + 1)
    random_counts = jax.random.randint(count_key, (STEPS, N_DOM, N_SPAN, R), 1, levels + 1)
    full_relation = jax.random.randint(full_key, (STEPS, N_DOM, 1, 1), 0, R)
    relation_ids = jnp.arange(R, dtype=jnp.int32).reshape(1, 1, 1, R)
    return jnp.where(relation_ids == full_relation, CAP, random_counts).astype(jnp.int32)


def with_ends(result, own_key, low, largest):
    extent = result.shape
    index_at = [jax.random.randint(jax.random.fold_in(own_key, axis), (), 0, extent[axis]) for axis in range(len(extent))]
    result = result.at[tuple(index_at)].set(low)
    longest = extent.index(max(extent))
    index_at[longest] = (index_at[longest] + 1) % extent[longest]
    return result.at[tuple(index_at)].set(largest)


def block_scale(key, shape, cuts, low, top_value):
    level, own = 1.0, jax.random.fold_in(key, 6)
    for axis_at, blocks in cuts:
        heights = jnp.exp(jax.random.uniform(jax.random.fold_in(own, axis_at), (blocks,), jnp.float32, low / len(cuts), top_value / len(cuts)))
        level = level * jnp.repeat(heights, shape[axis_at] // blocks).reshape([-1 if axis == axis_at else 1 for axis in range(len(shape))])
    return level


def bell_draw(rng, dims, deviation, limit, pieces=(), kind=jnp.bfloat16):
    drawn = jax.random.normal(rng, dims, jnp.float32) * deviation
    if len(pieces) > 0:
        drawn = block_scale(rng, dims, pieces, -0.22, 0.18) * drawn
    return jnp.clip(drawn, min=-limit, max=limit).astype(kind)


def setup_inputs(seed: int = 0) -> dict:
    key_of = jax.random.split(jax.random.key(seed), 7)
    entities = bell_draw(key_of[0], (ENT, D), 0.35, 2.5, ((0, 8),))
    operators = bell_draw(key_of[1], (R, D, D), D ** -0.5, 0.375, ((0, 4),))
    left_rows = with_ends(jax.random.randint(key_of[2], (STEPS, N_DOM, N_SPAN, SLOTS), 0, PART_ROWS), jax.random.fold_in(key_of[2], 1), 0, PART_ROWS - 1).astype(jnp.int32)
    right_rows = with_ends(jax.random.randint(key_of[3], (STEPS, N_DOM, N_SPAN, SLOTS), 0, PART_ROWS), jax.random.fold_in(key_of[3], 1), 0, PART_ROWS - 1).astype(jnp.int32)
    negatives = with_ends(jax.random.randint(key_of[4], (STEPS, N_DOM, N_SPAN, NEG), 0, PART_ROWS), jax.random.fold_in(key_of[4], 1), 0, PART_ROWS - 1).astype(jnp.int32)
    counts = draw_counts(jax.random.fold_in(key_of[6], 71), 0)
    return dict(entities=entities, operators=operators, left_rows=left_rows, right_rows=right_rows, negatives=negatives, counts=counts)


def live_slots(count_row):
    return (count_row[:, None] > jnp.arange(CAP, dtype=jnp.int32)[None, :]).astype(jnp.float32).reshape(-1)


def reference(entities, operators, left_rows, right_rows, negatives, counts):
    neg_scale = float(NEG) ** -0.5
    operators_wide = operators.astype(jnp.float32)

    def visit_bucket(totals, position):
        ent_grad, rel_grad = totals
        bucket = position // (N_DOM * N_SPAN)
        remainder = position % (N_DOM * N_SPAN)
        partition = remainder // N_SPAN
        group_id = remainder % N_SPAN
        right_part = (partition + bucket) % N_DOM
        left_index = left_rows[bucket, partition, group_id] + partition * PART_ROWS
        right_index = right_rows[bucket, partition, group_id] + right_part * PART_ROWS
        negative_index = negatives[bucket, partition, group_id] + right_part * PART_ROWS
        live_mask = live_slots(counts[bucket, partition, group_id])
        left_vecs = entities[left_index]
        right_vecs = entities[right_index]
        negative_vecs = entities[negative_index]
        queries = jnp.einsum("rkd,rde->rke", left_vecs.reshape(R, CAP, D).astype(jnp.float32), operators_wide)
        queries = queries.reshape(SLOTS, D).astype(jnp.bfloat16)
        queries_wide = queries.astype(jnp.float32)
        positive = jnp.sum(queries_wide * right_vecs.astype(jnp.float32), axis=1)
        scores = jnp.dot(queries, negative_vecs.T, preferred_element_type=jnp.float32)
        pos_grad = -live_mask * jax.nn.sigmoid(-positive)
        neg_grad = (live_mask[:, None] * jax.nn.sigmoid(scores) * neg_scale).astype(jnp.bfloat16)
        query_grad = pos_grad[:, None] * right_vecs.astype(jnp.float32) + jnp.dot(neg_grad, negative_vecs, preferred_element_type=jnp.float32)
        query_grad = query_grad.astype(jnp.bfloat16)
        grad_blocks = query_grad.reshape(R, CAP, D).astype(jnp.float32)
        left_grad = jnp.einsum("rke,rde->rkd", grad_blocks, operators_wide).reshape(SLOTS, D).astype(jnp.bfloat16)
        rel_grad = rel_grad + jnp.einsum("rkd,rke->rde", left_vecs.reshape(R, CAP, D).astype(jnp.float32), grad_blocks)
        negative_rows = jnp.dot(neg_grad.T, queries, preferred_element_type=jnp.float32)
        ent_grad = ent_grad.at[left_index].add(left_grad.astype(jnp.float32))
        ent_grad = ent_grad.at[right_index].add(pos_grad[:, None] * queries_wide)
        ent_grad = ent_grad.at[negative_index].add(negative_rows)
        return (ent_grad, rel_grad), None

    initial = (jnp.zeros((ENT, D), jnp.float32), jnp.zeros((R, D, D), jnp.float32))
    totals, _ = lax.scan(visit_bucket, initial, jnp.arange(STEPS * N_DOM * N_SPAN, dtype=jnp.int32))
    return totals[0], totals[1]
```

```python
import functools

import jax
import jax.numpy as jnp
from jax import lax
from jax.experimental import pallas as pl
from jax.experimental.pallas import tpu as pltpu
from jax.sharding import PartitionSpec as P

MESH = pl.DeviceIdType.MESH
F32 = jnp.float32
BF16 = jnp.bfloat16
LANES = 128
MULT_AT = 16


def dot(a, b, dims):
    return lax.dot_general(a, b, (dims, ((), ())), preferred_element_type=F32)


def rounded(value):
    return value.astype(BF16).astype(F32)


def kernel(
    dims,
    ent,
    ops,
    left_rows,
    right_rows,
    negatives,
    counts,
    ent_out,
    rel_out,
    slabs,
    meta_send,
    meta,
    cols,
    onehot,
    lefts,
    queries,
    query_grads,
    acc,
    own_grad,
    grad_send,
    grad_recv,
    home_send,
    home_recv,
    rel_acc,
    y_send,
    y_recv,
    z_send,
    z_recv,
    meta_ss,
    meta_rs,
    slab_ss,
    slab_rs,
    grad_ss,
    grad_rs,
    home_ss,
    home_rs,
    y_ss,
    y_rs,
    z_ss,
    z_rs,
):
    buckets, doms, groups, rel_own, cap, chunks = dims
    part_rows, width = ent.shape
    slot_count = left_rows.shape[1]
    neg_count = negatives.shape[1]
    relations = rel_own * groups
    slots = rel_own * cap
    levels = doms // 2
    own_rows = part_rows // groups
    out_rows = width // doms
    chunk_rels = rel_own // chunks
    chunk_rows = chunk_rels * out_rows
    mult_rows = part_rows // LANES
    neg_scale = float(neg_count) ** (-0.5)
    dom = lax.axis_index("dom")
    span = lax.axis_index("span")
    y = lax.rem(dom, 2)
    z = lax.div(dom, 2)

    def span_peer(offset):
        return (dom, lax.rem(span + offset, groups))

    def dom_peer(offset):
        return (lax.rem(dom + offset + doms, doms), span)

    def send(src, dst, send_sem, recv_sem, peer):
        copy = pltpu.make_async_remote_copy(
            src_ref=src,
            dst_ref=dst,
            send_sem=send_sem,
            recv_sem=recv_sem,
            device_id=peer,
            device_id_type=MESH,
        )
        copy.start()
        return copy

    barrier = pltpu.get_barrier_semaphore()
    for offset in range(1, groups):
        pl.semaphore_signal(barrier, inc=1, device_id=span_peer(offset), device_id_type=MESH)
    for offset in range(1, doms):
        pl.semaphore_signal(barrier, inc=1, device_id=dom_peer(offset), device_id_type=MESH)

    expand = (
        lax.broadcasted_iota(jnp.int32, (relations, slot_count), 1) // cap
        == lax.broadcasted_iota(jnp.int32, (relations, slot_count), 0)
    )
    wide_counts = dot(
        counts[...].astype(F32).astype(BF16),
        jnp.where(expand, 1.0, 0.0).astype(BF16),
        ((1,), (0,)),
    )
    place = (lax.broadcasted_iota(jnp.int32, (buckets, slot_count), 1) % cap).astype(F32)
    live = jnp.where(wide_counts > place, 1.0, 0.0)
    left_wide = left_rows[...].astype(F32)
    right_wide = right_rows[...].astype(F32)
    meta_send[...] = jnp.zeros(meta_send.shape, F32)
    for holder in range(groups):
        cut = slice(holder * slots, (holder + 1) * slots)
        meta_send[holder, 0:buckets, 0:slots] = left_wide[:, cut]
        meta_send[holder, buckets : 2 * buckets, 0:slots] = right_wide[:, cut]
        meta_send[holder, 2 * buckets : 3 * buckets, 0:slots] = live[:, cut]
    for bucket in range(buckets):
        row = negatives[bucket : bucket + 1, :]
        high = lax.broadcasted_iota(jnp.int32, (mult_rows, neg_count), 0) == row // LANES
        low = lax.broadcasted_iota(jnp.int32, (LANES, neg_count), 0) == row % LANES
        mult = dot(
            jnp.where(high, 1.0, 0.0).astype(BF16),
            jnp.where(low, 1.0, 0.0).astype(BF16),
            ((1,), (1,)),
        )
        at = MULT_AT + bucket * mult_rows
        for holder in range(groups):
            meta_send[holder, at : at + mult_rows, :] = mult

    pl.semaphore_wait(barrier, groups - 1 + doms - 1)
    meta_copies = []
    for offset in range(1, groups):
        peer = span_peer(offset)
        meta_copies.append(
            send(meta_send.at[peer[1]], meta.at[offset], meta_ss.at[offset], meta_rs.at[offset], peer)
        )
    slab_copies = [
        send(ent, slabs.at[b - 1], slab_ss.at[b - 1], slab_rs.at[b - 1], dom_peer(-b))
        for b in range(1, buckets)
    ]
    meta[0] = meta_send[span]
    for copy in meta_copies:
        copy.wait()

    lane_row = lax.broadcasted_iota(jnp.int32, (slots, part_rows), 1).astype(F32)
    for group in range(groups):
        cols[group] = jnp.transpose(meta[group, 0:MULT_AT, :])
    for bucket in range(buckets):
        for group in range(groups):
            hit = lane_row == cols[group, 0:slots, bucket : bucket + 1]
            onehot[bucket, group * slots : (group + 1) * slots, :] = jnp.where(hit, 1.0, 0.0).astype(BF16)
        picked = dot(onehot[bucket], ent[...], ((1,), (0,)))
        for group in range(groups):
            at = (bucket * groups + group) * cap
            lefts[:, at : at + cap, :] = picked[group * slots : (group + 1) * slots].reshape(rel_own, cap, width)

    def apply_operator(rel, _):
        queries[rel] = rounded(dot(lefts[rel].astype(BF16), ops[rel], ((1,), (0,))))
        return _

    lax.fori_loop(0, rel_own, apply_operator, 0)

    acc[...] = jnp.zeros(acc.shape, F32)

    def score(bucket, right):
        def one_group(group, _):
            at = pl.multiple_of((bucket * groups + group) * cap, cap)
            query = queries[:, pl.ds(at, cap), :].reshape(slots, width).astype(BF16)
            right_col = cols[group, 0:slots, buckets + bucket : buckets + bucket + 1]
            live_col = cols[group, 0:slots, 2 * buckets + bucket : 2 * buckets + bucket + 1]
            first = MULT_AT + bucket * mult_rows
            mult = jnp.concatenate(
                [meta[group, first + part : first + part + 1, :] for part in range(mult_rows)], axis=1
            )
            scores = dot(query, right[...], ((1,), (1,)))
            hit = lane_row == right_col
            positive = jnp.sum(jnp.where(hit, scores, 0.0), axis=1, keepdims=True)
            pos_grad = -live_col * jax.nn.sigmoid(-positive)
            neg_grad = rounded((jnp.tanh(scores * 0.5) + 1.0) * (live_col * (0.5 * neg_scale)))
            weight = neg_grad * mult + jnp.where(hit, pos_grad, 0.0)
            high = weight.astype(BF16)
            low = (weight - high.astype(F32)).astype(BF16)
            both = jnp.concatenate([high, low], axis=0)
            parts = dot(both, right[...], ((1,), (0,)))
            query_grad = rounded(parts[0:slots] + parts[slots:])
            query_grads[:, pl.ds(at, cap), :] = query_grad.reshape(rel_own, cap, width)
            twice = jnp.concatenate([query, query], axis=0)
            acc[bucket] += dot(twice, both, ((0,), (0,)))
            return _

        lax.fori_loop(0, groups, one_group, 0)

    def send_grads(bucket):
        total = jnp.transpose(acc[bucket])
        own_grad[bucket] = total
        for holder in range(groups):
            grad_send[bucket, holder] = total[holder * own_rows : (holder + 1) * own_rows].astype(BF16)
        copies = []
        for offset in range(1, groups):
            peer = span_peer(offset)
            copies.append(
                send(
                    grad_send.at[bucket, peer[1]],
                    grad_recv.at[bucket, offset],
                    grad_ss.at[bucket, offset],
                    grad_rs.at[bucket, offset],
                    peer,
                )
            )
        return copies

    def gathered(bucket, copies):
        for copy in copies:
            copy.wait()
        total = own_grad[bucket, pl.ds(pl.multiple_of(span * own_rows, own_rows), own_rows), :]
        for offset in range(1, groups):
            total = total + grad_recv[bucket, offset].astype(F32)
        return total

    score(0, ent)
    grad_copies = [None]
    for bucket in range(1, buckets):
        slab_copies[bucket - 1].wait()
        score(bucket, slabs.at[bucket - 1])

    y_copies = []
    for chunk in range(chunks):

        def one_relation(rel, _):
            outer = dot(lefts[rel].astype(BF16), query_grads[rel].astype(BF16), ((0,), (0,)))
            at = pl.multiple_of(rel * out_rows, out_rows)
            for level in range(levels):
                for side in range(2):
                    first = (level * 2 + side) * out_rows
                    rel_acc[side, level, pl.ds(at, out_rows), :] = outer[first : first + out_rows]
            return _

        lax.fori_loop(chunk * chunk_rels, (chunk + 1) * chunk_rels, one_relation, 0)
        rows = slice(chunk * chunk_rows, (chunk + 1) * chunk_rows)
        y_send[chunk] = rel_acc[1 - y, :, rows, :].astype(BF16)
        y_copies.append(
            send(y_send.at[chunk], y_recv.at[chunk], y_ss.at[chunk], y_rs.at[chunk], (dom + 1 - 2 * y, span))
        )

    for bucket in range(1, buckets):
        grad_copies.append(send_grads(bucket))

    def apply_transposed(rel, _):
        queries[rel] = rounded(dot(query_grads[rel].astype(BF16), ops[rel], ((1,), (1,))))
        return _

    lax.fori_loop(0, rel_own, apply_transposed, 0)

    z_copies = []

    def send_level(chunk):
        y_copies[chunk].wait()
        rows = slice(chunk * chunk_rows, (chunk + 1) * chunk_rows)
        total = rel_acc[y, :, rows, :] + y_recv[chunk].astype(F32)
        rel_acc[y, :, rows, :] = total
        z_send[chunk] = total.astype(BF16)
        for offset in range(1, levels):
            level = lax.rem(z + offset, levels)
            z_copies.append(
                send(
                    z_send.at[chunk, level],
                    z_recv.at[chunk, offset],
                    z_ss.at[chunk, offset],
                    z_rs.at[chunk, offset],
                    (level * 2 + y, span),
                )
            )

    send_level(0)
    for bucket in range(buckets):
        grad_rows = jnp.concatenate(
            [
                queries[:, (bucket * groups + group) * cap : (bucket * groups + group + 1) * cap, :].reshape(slots, width)
                for group in range(groups)
            ],
            axis=0,
        ).astype(BF16)
        acc[0] += dot(grad_rows, onehot[bucket], ((0,), (0,)))
    grad_copies[0] = send_grads(0)
    send_level(1)

    home_copies = []
    for bucket in range(1, buckets):
        home_send[bucket] = gathered(bucket, grad_copies[bucket])
        home_copies.append(
            send(home_send.at[bucket], home_recv.at[bucket], home_ss.at[bucket], home_rs.at[bucket], dom_peer(bucket))
        )
    for chunk in range(2, chunks):
        send_level(chunk)

    total = gathered(0, grad_copies[0])
    for bucket in range(1, buckets):
        home_copies[bucket - 1].wait()
        total = total + home_recv[bucket]
    ent_out[...] = total

    for chunk in range(chunks):
        for copy in z_copies[chunk * (levels - 1) : (chunk + 1) * (levels - 1)]:
            copy.wait()
        rows = slice(chunk * chunk_rows, (chunk + 1) * chunk_rows)
        total = rel_acc[y, z, rows, :]
        for offset in range(1, levels):
            total = total + z_recv[chunk, offset].astype(F32)
        rel_out[rows, :] = total


def shards(entities, operators, left_rows, right_rows, negatives, counts):
    buckets = left_rows.shape[0]
    slot_count = left_rows.shape[-1]
    neg_count = negatives.shape[-1]
    groups = lax.axis_size("span")
    doms = lax.axis_size("dom")
    rel_own = operators.shape[0]
    relations = rel_own * groups
    cap = slot_count // relations
    slots = rel_own * cap
    part_rows, width = entities.shape
    own_rows = part_rows // groups
    out_rows = width // doms
    levels = doms // 2
    chunks = 4 if (rel_own // 4) * out_rows % 16 == 0 else 2
    chunk_rows = rel_own // chunks * out_rows
    mult_rows = part_rows // LANES
    meta_rows = MULT_AT + -(-buckets * mult_rows // 8) * 8
    edges = buckets * groups * cap
    dims = (buckets, doms, groups, rel_own, cap, chunks)
    dma = pltpu.SemaphoreType.DMA
    vmem = pl.BlockSpec(memory_space=pltpu.VMEM)
    ent_grad, rel_grad = pl.pallas_call(
        functools.partial(kernel, dims),
        out_shape=(
            jax.ShapeDtypeStruct((own_rows, width), F32),
            jax.ShapeDtypeStruct((rel_own * out_rows, width), F32),
        ),
        in_specs=[vmem] * 6,
        out_specs=(vmem, vmem),
        scratch_shapes=[
            pltpu.VMEM((buckets - 1, part_rows, width), BF16),
            pltpu.VMEM((groups, meta_rows, LANES), F32),
            pltpu.VMEM((groups, meta_rows, LANES), F32),
            pltpu.VMEM((groups, LANES, MULT_AT), F32),
            pltpu.VMEM((buckets, groups * slots, part_rows), BF16),
            pltpu.VMEM((rel_own, edges, width), F32),
            pltpu.VMEM((rel_own, edges, width), F32),
            pltpu.VMEM((rel_own, edges, width), F32),
            pltpu.VMEM((buckets, width, part_rows), F32),
            pltpu.VMEM((buckets, part_rows, width), F32),
            pltpu.VMEM((buckets, groups, own_rows, width), BF16),
            pltpu.VMEM((buckets, groups, own_rows, width), BF16),
            pltpu.VMEM((buckets, own_rows, width), F32),
            pltpu.VMEM((buckets, own_rows, width), F32),
            pltpu.VMEM((2, levels, rel_own * out_rows, width), F32),
            pltpu.VMEM((chunks, levels, chunk_rows, width), BF16),
            pltpu.VMEM((chunks, levels, chunk_rows, width), BF16),
            pltpu.VMEM((chunks, levels, chunk_rows, width), BF16),
            pltpu.VMEM((chunks, levels, chunk_rows, width), BF16),
            dma((groups,)),
            dma((groups,)),
            dma((buckets - 1,)),
            dma((buckets - 1,)),
            dma((buckets, groups)),
            dma((buckets, groups)),
            dma((buckets,)),
            dma((buckets,)),
            dma((chunks,)),
            dma((chunks,)),
            dma((chunks, levels)),
            dma((chunks, levels)),
        ],
        compiler_params=pltpu.CompilerParams(
            collective_id=0, has_side_effects=True, vmem_limit_bytes=58 * 1024 * 1024
        ),
        name="train_step",
    )(
        entities,
        operators,
        left_rows.reshape(buckets, slot_count),
        right_rows.reshape(buckets, slot_count),
        negatives.reshape(buckets, neg_count),
        counts.reshape(buckets, relations),
    )
    return (ent_grad, rel_grad.reshape(rel_own, out_rows, width))


def solution(mesh):
    in_specs = (
        P("dom", None),
        P("span", None, None),
        P(None, "dom", "span", None),
        P(None, "dom", "span", None),
        P(None, "dom", "span", None),
        P(None, "dom", "span", None),
    )
    out_specs = (P(("dom", "span"), None), P("span", "dom", None))
    return jax.shard_map(shards, mesh=mesh, in_specs=in_specs, out_specs=out_specs, check_vma=False)
```

```python
import functools

import jax
import jax.numpy as jnp
from jax import lax
from jax.experimental import pallas as pl
from jax.experimental.pallas import tpu as pltpu
from jax.sharding import PartitionSpec as P

MESH = pl.DeviceIdType.MESH
F32 = jnp.float32
BF16 = jnp.bfloat16
LANES = 128
MULT_AT = 16


def dot(a, b, dims):
    return lax.dot_general(a, b, (dims, ((), ())), preferred_element_type=F32)


def rounded(value):
    return value.astype(BF16).astype(F32)


def kernel(
    dims,
    ent,
    ops,
    left_rows,
    right_rows,
    negatives,
    counts,
    ent_out,
    rel_out,
    slabs,
    meta_send,
    meta,
    cols,
    times,
    onehot,
    lefts,
    queries,
    query_grads,
    acc,
    own_grad,
    grad_send,
    grad_recv,
    home_send,
    home_recv,
    rel_acc,
    y_send,
    y_recv,
    z_send,
    z_recv,
    meta_ss,
    meta_rs,
    slab_ss,
    slab_rs,
    grad_ss,
    grad_rs,
    home_ss,
    home_rs,
    y_ss,
    y_rs,
    z_ss,
    z_rs,
):
    buckets, doms, groups, rel_own, cap, chunks = dims
    part_rows, width = ent.shape
    slot_count = left_rows.shape[-1]
    neg_count = negatives.shape[-1]
    relations = rel_own * groups
    slots = rel_own * cap
    levels = doms // 2
    own_rows = part_rows // groups
    out_rows = width // doms
    chunk_rels = rel_own // chunks
    chunk_rows = chunk_rels * out_rows
    share = groups * cap
    block = chunk_rels * share
    mult_rows = part_rows // LANES
    neg_scale = float(neg_count) ** (-0.5)
    dom = lax.axis_index("dom")
    span = lax.axis_index("span")
    y = lax.rem(dom, 2)
    z = lax.div(dom, 2)

    def span_peer(offset):
        return (dom, lax.rem(span + offset, groups))

    def dom_peer(offset):
        return (lax.rem(dom + offset + doms, doms), span)

    def send(src, dst, send_sem, recv_sem, peer):
        copy = pltpu.make_async_remote_copy(
            src_ref=src,
            dst_ref=dst,
            send_sem=send_sem,
            recv_sem=recv_sem,
            device_id=peer,
            device_id_type=MESH,
        )
        copy.start()
        return copy

    barrier = pltpu.get_barrier_semaphore()
    for offset in range(1, groups):
        pl.semaphore_signal(barrier, inc=1, device_id=span_peer(offset), device_id_type=MESH)
    for offset in range(1, doms):
        pl.semaphore_signal(barrier, inc=1, device_id=dom_peer(offset), device_id_type=MESH)

    def rows_of(ref):
        return jnp.concatenate([ref[bucket, 0] for bucket in range(buckets)], axis=0)

    expand = (
        lax.broadcasted_iota(jnp.int32, (relations, slot_count), 1) // cap
        == lax.broadcasted_iota(jnp.int32, (relations, slot_count), 0)
    )
    wide_counts = dot(
        rows_of(counts).astype(F32).astype(BF16),
        jnp.where(expand, 1.0, 0.0).astype(BF16),
        ((1,), (0,)),
    )
    place = (lax.broadcasted_iota(jnp.int32, (buckets, slot_count), 1) % cap).astype(F32)
    live = jnp.where(wide_counts > place, 1.0, 0.0)
    left_wide = rows_of(left_rows).astype(F32)
    right_wide = rows_of(right_rows).astype(F32)
    meta_send[...] = jnp.zeros(meta_send.shape, F32)
    for holder in range(groups):
        cut = slice(holder * slots, (holder + 1) * slots)
        meta_send[holder, 0:buckets, 0:slots] = left_wide[:, cut]
        meta_send[holder, buckets : 2 * buckets, 0:slots] = right_wide[:, cut]
        meta_send[holder, 2 * buckets : 3 * buckets, 0:slots] = live[:, cut]
    for bucket in range(buckets):
        row = negatives[bucket, 0]
        high = lax.broadcasted_iota(jnp.int32, (mult_rows, neg_count), 0) == row // LANES
        low = lax.broadcasted_iota(jnp.int32, (LANES, neg_count), 0) == row % LANES
        mult = dot(
            jnp.where(high, 1.0, 0.0).astype(BF16),
            jnp.where(low, 1.0, 0.0).astype(BF16),
            ((1,), (1,)),
        )
        at = MULT_AT + bucket * mult_rows
        for holder in range(groups):
            meta_send[holder, at : at + mult_rows, :] = mult

    pl.semaphore_wait(barrier, groups - 1 + doms - 1)
    meta_copies = []
    for offset in range(1, groups):
        peer = span_peer(offset)
        meta_copies.append(
            send(meta_send.at[peer[1]], meta.at[offset], meta_ss.at[offset], meta_rs.at[offset], peer)
        )
    slab_copies = [
        send(ent, slabs.at[b - 1], slab_ss.at[b - 1], slab_rs.at[b - 1], dom_peer(-b))
        for b in range(1, buckets)
    ]
    meta[0] = meta_send[span]
    for copy in meta_copies:
        copy.wait()

    lane_row = lax.broadcasted_iota(jnp.int32, (block, part_rows), 1).astype(F32)
    for group in range(groups):
        turned = jnp.transpose(meta[group, 0:MULT_AT, :])
        cols[:, group * cap : (group + 1) * cap, :] = turned[0:slots].reshape(rel_own, cap, MULT_AT)
        for bucket in range(buckets):
            first = MULT_AT + bucket * mult_rows
            mult = jnp.concatenate(
                [meta[group, first + part : first + part + 1, :] for part in range(mult_rows)], axis=1
            )
            times[bucket, group * cap : (group + 1) * cap, :] = jnp.broadcast_to(mult, (cap, part_rows))

    def column(chunk, which):
        held = cols[chunk * chunk_rels : (chunk + 1) * chunk_rels].reshape(block, MULT_AT)
        return held[:, which : which + 1]

    for bucket in range(buckets):
        for chunk in range(chunks):
            hit = lane_row == column(chunk, bucket)
            onehot[bucket, chunk * block : (chunk + 1) * block, :] = jnp.where(hit, 1.0, 0.0).astype(BF16)
        picked = dot(onehot[bucket], ent[...], ((1,), (0,)))
        lefts[:, bucket * share : (bucket + 1) * share, :] = picked.reshape(rel_own, share, width)
    for rel in range(rel_own):
        queries[rel] = rounded(dot(lefts[rel].astype(BF16), ops[rel], ((1,), (0,))))

    def score(chunk, bucket):
        right = ent if bucket == 0 else slabs.at[bucket - 1]
        rels = slice(chunk * chunk_rels, (chunk + 1) * chunk_rels)
        at = slice(bucket * share, (bucket + 1) * share)
        query = queries[rels, at, :].reshape(block, width).astype(BF16)
        live_col = column(chunk, 2 * buckets + bucket)
        scores = dot(query, right[...], ((1,), (1,)))
        hit = lane_row == column(chunk, buckets + bucket)
        positive = jnp.sum(jnp.where(hit, scores, 0.0), axis=1, keepdims=True)
        pos_grad = -live_col * jax.nn.sigmoid(-positive)
        neg_grad = rounded((jnp.tanh(scores * 0.5) + 1.0) * (live_col * (0.5 * neg_scale)))
        counted = neg_grad.reshape(chunk_rels, share, part_rows) * times[bucket][None]
        weight = counted.reshape(block, part_rows) + jnp.where(hit, pos_grad, 0.0)
        high = weight.astype(BF16)
        low = (weight - high.astype(F32)).astype(BF16)
        both = jnp.concatenate([high, low], axis=0)
        parts = dot(both, right[...], ((1,), (0,)))
        query_grad = rounded(parts[0:block] + parts[block:])
        query_grads[rels, at, :] = query_grad.reshape(chunk_rels, share, width)
        twice = jnp.concatenate([query, query], axis=0)
        slab_grad = dot(twice, both, ((0,), (0,)))
        if chunk == 0:
            acc[bucket] = slab_grad
        else:
            acc[bucket] += slab_grad

    y_copies = []

    def send_pair(chunk):
        for rel in range(chunk * chunk_rels, (chunk + 1) * chunk_rels):
            outer = dot(lefts[rel].astype(BF16), query_grads[rel].astype(BF16), ((0,), (0,)))
            for level in range(levels):
                for side in range(2):
                    first = (level * 2 + side) * out_rows
                    rel_acc[side, level, rel * out_rows : (rel + 1) * out_rows, :] = outer[first : first + out_rows]
        rows = slice(chunk * chunk_rows, (chunk + 1) * chunk_rows)
        y_send[chunk] = rel_acc[1 - y, :, rows, :].astype(BF16)
        y_copies.append(
            send(y_send.at[chunk], y_recv.at[chunk], y_ss.at[chunk], y_rs.at[chunk], (dom + 1 - 2 * y, span))
        )

    z_copies = []

    def send_level(chunk):
        y_copies[chunk].wait()
        rows = slice(chunk * chunk_rows, (chunk + 1) * chunk_rows)
        total = rel_acc[y, :, rows, :] + y_recv[chunk].astype(F32)
        rel_acc[y, :, rows, :] = total
        z_send[chunk] = total.astype(BF16)
        for offset in range(1, levels):
            level = lax.rem(z + offset, levels)
            z_copies.append(
                send(
                    z_send.at[chunk, level],
                    z_recv.at[chunk, offset],
                    z_ss.at[chunk, offset],
                    z_rs.at[chunk, offset],
                    (level * 2 + y, span),
                )
            )

    def left_part(chunk):
        rels = range(chunk * chunk_rels, (chunk + 1) * chunk_rels)
        turned = [rounded(dot(query_grads[rel].astype(BF16), ops[rel], ((1,), (1,)))) for rel in rels]
        rows, marks = [], []
        for bucket in range(buckets):
            rows += [value[bucket * share : (bucket + 1) * share] for value in turned]
            marks.append(onehot[bucket, chunk * block : (chunk + 1) * block, :])
        rows = jnp.concatenate(rows, axis=0).astype(BF16)
        acc[0] += dot(rows, jnp.concatenate(marks, axis=0), ((0,), (0,)))

    def send_grads(bucket):
        total = jnp.transpose(acc[bucket])
        own_grad[bucket] = total
        for holder in range(groups):
            grad_send[bucket, holder] = total[holder * own_rows : (holder + 1) * own_rows].astype(BF16)
        copies = []
        for offset in range(1, groups):
            peer = span_peer(offset)
            copies.append(
                send(
                    grad_send.at[bucket, peer[1]],
                    grad_recv.at[bucket, offset],
                    grad_ss.at[bucket, offset],
                    grad_rs.at[bucket, offset],
                    peer,
                )
            )
        return copies

    def gathered(bucket, copies):
        for copy in copies:
            copy.wait()
        total = own_grad[bucket, pl.ds(pl.multiple_of(span * own_rows, own_rows), own_rows), :]
        for offset in range(1, groups):
            total = total + grad_recv[bucket, offset].astype(F32)
        return total

    score(0, 0)
    score(1, 0)
    for copy in slab_copies:
        copy.wait()
    for chunk in range(chunks):
        if chunk > 1:
            score(chunk, 0)
        for bucket in range(1, buckets):
            score(chunk, bucket)
        send_pair(chunk)
        if chunk > 0:
            send_level(chunk - 1)
        if chunk < chunks - 1:
            left_part(chunk)
    grad_copies = [None] + [send_grads(bucket) for bucket in range(1, buckets)]
    left_part(chunks - 1)
    grad_copies[0] = send_grads(0)
    send_level(chunks - 1)

    home_copies = []
    for bucket in range(1, buckets):
        home_send[bucket] = gathered(bucket, grad_copies[bucket])
        home_copies.append(
            send(home_send.at[bucket], home_recv.at[bucket], home_ss.at[bucket], home_rs.at[bucket], dom_peer(bucket))
        )
    total = gathered(0, grad_copies[0])
    for bucket in range(1, buckets):
        home_copies[bucket - 1].wait()
        total = total + home_recv[bucket]
    ent_out[...] = total

    for chunk in range(chunks):
        for copy in z_copies[chunk * (levels - 1) : (chunk + 1) * (levels - 1)]:
            copy.wait()
        rows = slice(chunk * chunk_rows, (chunk + 1) * chunk_rows)
        total = rel_acc[y, z, rows, :]
        for offset in range(1, levels):
            total = total + z_recv[chunk, offset].astype(F32)
        rel_out[rows, :] = total


def hand_over(ent_grad, rel_grad, ent_out, rel_out, sems):
    copies = [
        pltpu.make_async_copy(ent_grad, ent_out, sems.at[0]),
        pltpu.make_async_copy(rel_grad, rel_out, sems.at[1]),
    ]
    for copy in copies:
        copy.start()
    for copy in copies:
        copy.wait()


def shards(entities, operators, left_rows, right_rows, negatives, counts):
    buckets = left_rows.shape[0]
    slot_count = left_rows.shape[-1]
    neg_count = negatives.shape[-1]
    groups = lax.axis_size("span")
    doms = lax.axis_size("dom")
    rel_own = operators.shape[0]
    cap = slot_count // (rel_own * groups)
    slots = rel_own * cap
    part_rows, width = entities.shape
    own_rows = part_rows // groups
    out_rows = width // doms
    levels = doms // 2
    chunks = 4 if (rel_own // 4) * out_rows % 16 == 0 else 2
    chunk_rows = rel_own // chunks * out_rows
    mult_rows = part_rows // LANES
    meta_rows = MULT_AT + -(-buckets * mult_rows // 8) * 8
    edges = buckets * groups * cap
    dims = (buckets, doms, groups, rel_own, cap, chunks)
    dma = pltpu.SemaphoreType.DMA
    vmem = pl.BlockSpec(memory_space=pltpu.VMEM)
    ent_grad, rel_grad = pl.pallas_call(
        functools.partial(kernel, dims),
        out_shape=(
            jax.ShapeDtypeStruct((own_rows, width), F32),
            jax.ShapeDtypeStruct((rel_own * out_rows, width), F32),
        ),
        in_specs=[vmem] * 6,
        out_specs=(vmem, vmem),
        scratch_shapes=[
            pltpu.VMEM((buckets - 1, part_rows, width), BF16),
            pltpu.VMEM((groups, meta_rows, LANES), F32),
            pltpu.VMEM((groups, meta_rows, LANES), F32),
            pltpu.VMEM((rel_own, groups * cap, MULT_AT), F32),
            pltpu.VMEM((buckets, groups * cap, part_rows), F32),
            pltpu.VMEM((buckets, groups * slots, part_rows), BF16),
            pltpu.VMEM((rel_own, edges, width), F32),
            pltpu.VMEM((rel_own, edges, width), F32),
            pltpu.VMEM((rel_own, edges, width), F32),
            pltpu.VMEM((buckets, width, part_rows), F32),
            pltpu.VMEM((buckets, part_rows, width), F32),
            pltpu.VMEM((buckets, groups, own_rows, width), BF16),
            pltpu.VMEM((buckets, groups, own_rows, width), BF16),
            pltpu.VMEM((buckets, own_rows, width), F32),
            pltpu.VMEM((buckets, own_rows, width), F32),
            pltpu.VMEM((2, levels, rel_own * out_rows, width), F32),
            pltpu.VMEM((chunks, levels, chunk_rows, width), BF16),
            pltpu.VMEM((chunks, levels, chunk_rows, width), BF16),
            pltpu.VMEM((chunks, levels, chunk_rows, width), BF16),
            pltpu.VMEM((chunks, levels, chunk_rows, width), BF16),
            dma((groups,)),
            dma((groups,)),
            dma((buckets - 1,)),
            dma((buckets - 1,)),
            dma((buckets, groups)),
            dma((buckets, groups)),
            dma((buckets,)),
            dma((buckets,)),
            dma((chunks,)),
            dma((chunks,)),
            dma((chunks, levels)),
            dma((chunks, levels)),
        ],
        compiler_params=pltpu.CompilerParams(
            collective_id=0, has_side_effects=True, vmem_limit_bytes=58 * 1024 * 1024
        ),
        name="train_step",
    )(entities, operators, left_rows, right_rows, negatives, counts)
    anywhere = pl.BlockSpec(memory_space=pl.ANY)
    ent_grad, rel_grad = pl.pallas_call(
        hand_over,
        out_shape=(
            jax.ShapeDtypeStruct(ent_grad.shape, F32),
            jax.ShapeDtypeStruct(rel_grad.shape, F32),
        ),
        in_specs=[anywhere] * 2,
        out_specs=(anywhere, anywhere),
        scratch_shapes=[dma((2,))],
        compiler_params=pltpu.CompilerParams(vmem_limit_bytes=58 * 1024 * 1024),
        name="hand_over",
    )(ent_grad, rel_grad)
    return (ent_grad, rel_grad.reshape(rel_own, out_rows, width))


def solution(mesh):
    in_specs = (
        P("dom", None),
        P("span", None, None),
        P(None, "dom", "span", None),
        P(None, "dom", "span", None),
        P(None, "dom", "span", None),
        P(None, "dom", "span", None),
    )
    out_specs = (P(("dom", "span"), None), P("span", "dom", None))
    return jax.shard_map(shards, mesh=mesh, in_specs=in_specs, out_specs=out_specs, check_vma=False)
```

```python
import functools

import jax
import jax.numpy as jnp
from jax import lax
from jax.experimental import pallas as pl
from jax.experimental.pallas import tpu as pltpu
from jax.sharding import PartitionSpec as P

MESH = pl.DeviceIdType.MESH
F32 = jnp.float32
BF16 = jnp.bfloat16
LANES = 128
MULT_AT = 16


def dot(a, b, dims):
    return lax.dot_general(a, b, (dims, ((), ())), preferred_element_type=F32)


def rounded(value):
    return value.astype(BF16).astype(F32)


def kernel(
    dims,
    ent,
    ops,
    left_rows,
    right_rows,
    negatives,
    counts,
    ent_out,
    rel_out,
    slabs,
    meta_send,
    meta,
    cols,
    times,
    onehot,
    lefts,
    queries,
    query_grads,
    acc,
    own_grad,
    grad_send,
    grad_recv,
    home_send,
    home_recv,
    rel_acc,
    y_send,
    y_recv,
    z_send,
    z_recv,
    meta_ss,
    meta_rs,
    slab_ss,
    slab_rs,
    grad_ss,
    grad_rs,
    home_ss,
    home_rs,
    y_ss,
    y_rs,
    z_ss,
    z_rs,
):
    buckets, doms, groups, rel_own, cap, chunks = dims
    part_rows, width = ent.shape
    slot_count = left_rows.shape[-1]
    neg_count = negatives.shape[-1]
    relations = rel_own * groups
    slots = rel_own * cap
    levels = doms // 2
    own_rows = part_rows // groups
    out_rows = width // doms
    chunk_rels = rel_own // chunks
    chunk_rows = chunk_rels * out_rows
    share = groups * cap
    block = chunk_rels * share
    mult_rows = part_rows // LANES
    neg_scale = float(neg_count) ** (-0.5)
    dom = lax.axis_index("dom")
    span = lax.axis_index("span")
    y = lax.rem(dom, 2)
    z = lax.div(dom, 2)

    def span_peer(offset):
        return (dom, lax.rem(span + offset, groups))

    def dom_peer(offset):
        return (lax.rem(dom + offset + doms, doms), span)

    def send(src, dst, send_sem, recv_sem, peer):
        copy = pltpu.make_async_remote_copy(
            src_ref=src,
            dst_ref=dst,
            send_sem=send_sem,
            recv_sem=recv_sem,
            device_id=peer,
            device_id_type=MESH,
        )
        copy.start()
        return copy

    barrier = pltpu.get_barrier_semaphore()
    for offset in range(1, groups):
        pl.semaphore_signal(barrier, inc=1, device_id=span_peer(offset), device_id_type=MESH)
    for offset in range(1, doms):
        pl.semaphore_signal(barrier, inc=1, device_id=dom_peer(offset), device_id_type=MESH)

    def rows_of(ref):
        return jnp.concatenate([ref[bucket, 0] for bucket in range(buckets)], axis=0)

    expand = (
        lax.broadcasted_iota(jnp.int32, (relations, slot_count), 1) // cap
        == lax.broadcasted_iota(jnp.int32, (relations, slot_count), 0)
    )
    wide_counts = dot(
        rows_of(counts).astype(F32).astype(BF16),
        jnp.where(expand, 1.0, 0.0).astype(BF16),
        ((1,), (0,)),
    )
    place = (lax.broadcasted_iota(jnp.int32, (buckets, slot_count), 1) % cap).astype(F32)
    live = jnp.where(wide_counts > place, 1.0, 0.0)
    left_wide = rows_of(left_rows).astype(F32)
    right_wide = rows_of(right_rows).astype(F32)
    meta_send[...] = jnp.zeros(meta_send.shape, F32)
    for holder in range(groups):
        cut = slice(holder * slots, (holder + 1) * slots)
        meta_send[holder, 0:buckets, 0:slots] = left_wide[:, cut]
        meta_send[holder, buckets : 2 * buckets, 0:slots] = right_wide[:, cut]
        meta_send[holder, 2 * buckets : 3 * buckets, 0:slots] = live[:, cut]
    for bucket in range(buckets):
        row = negatives[bucket, 0]
        high = lax.broadcasted_iota(jnp.int32, (mult_rows, neg_count), 0) == row // LANES
        low = lax.broadcasted_iota(jnp.int32, (LANES, neg_count), 0) == row % LANES
        mult = dot(
            jnp.where(high, 1.0, 0.0).astype(BF16),
            jnp.where(low, 1.0, 0.0).astype(BF16),
            ((1,), (1,)),
        )
        at = MULT_AT + bucket * mult_rows
        for holder in range(groups):
            meta_send[holder, at : at + mult_rows, :] = mult

    pl.semaphore_wait(barrier, groups - 1 + doms - 1)
    meta_copies = []
    for offset in range(1, groups):
        peer = span_peer(offset)
        meta_copies.append(
            send(meta_send.at[peer[1]], meta.at[offset], meta_ss.at[offset], meta_rs.at[offset], peer)
        )
    part = pl.ds(pl.multiple_of(span * own_rows, own_rows), own_rows)
    slab_parts = [
        send(ent.at[part], slabs.at[b - 1, part], slab_ss.at[b - 1, 0], slab_rs.at[b - 1, 0], dom_peer(-b))
        for b in range(1, buckets)
    ]
    meta[0] = meta_send[span]
    for copy in meta_copies:
        copy.wait()

    lane_row = lax.broadcasted_iota(jnp.int32, (block, part_rows), 1).astype(F32)
    for group in range(groups):
        turned = jnp.transpose(meta[group, 0:MULT_AT, :])
        cols[:, group * cap : (group + 1) * cap, :] = turned[0:slots].reshape(rel_own, cap, MULT_AT)
        for bucket in range(buckets):
            first = MULT_AT + bucket * mult_rows
            mult = jnp.concatenate(
                [meta[group, first + part : first + part + 1, :] for part in range(mult_rows)], axis=1
            )
            times[bucket, group * cap : (group + 1) * cap, :] = jnp.broadcast_to(mult, (cap, part_rows))

    def column(chunk, which):
        held = cols[chunk * chunk_rels : (chunk + 1) * chunk_rels].reshape(block, MULT_AT)
        return held[:, which : which + 1]

    for bucket in range(buckets):
        for chunk in range(chunks):
            hit = lane_row == column(chunk, bucket)
            onehot[bucket, chunk * block : (chunk + 1) * block, :] = jnp.where(hit, 1.0, 0.0).astype(BF16)
        picked = dot(onehot[bucket], ent[...], ((1,), (0,)))
        lefts[:, bucket * share : (bucket + 1) * share, :] = picked.reshape(rel_own, share, width)
    slab_copies = []
    for b in range(1, buckets):
        slab_parts[b - 1].wait()
        for offset in range(1, groups):
            slab_copies.append(
                send(
                    slabs.at[b - 1, part],
                    slabs.at[b - 1, part],
                    slab_ss.at[b - 1, offset],
                    slab_rs.at[b - 1, offset],
                    span_peer(offset),
                )
            )
    for rel in range(rel_own):
        queries[rel] = rounded(dot(lefts[rel].astype(BF16), ops[rel], ((1,), (0,))))

    def score(chunk, bucket):
        right = ent if bucket == 0 else slabs.at[bucket - 1]
        rels = slice(chunk * chunk_rels, (chunk + 1) * chunk_rels)
        at = slice(bucket * share, (bucket + 1) * share)
        query = queries[rels, at, :].reshape(block, width).astype(BF16)
        live_col = column(chunk, 2 * buckets + bucket)
        scores = dot(query, right[...], ((1,), (1,)))
        hit = lane_row == column(chunk, buckets + bucket)
        positive = jnp.sum(jnp.where(hit, scores, 0.0), axis=1, keepdims=True)
        pos_grad = -live_col * jax.nn.sigmoid(-positive)
        neg_grad = rounded((jnp.tanh(scores * 0.5) + 1.0) * (live_col * (0.5 * neg_scale)))
        counted = neg_grad.reshape(chunk_rels, share, part_rows) * times[bucket][None]
        weight = counted.reshape(block, part_rows) + jnp.where(hit, pos_grad, 0.0)
        high = weight.astype(BF16)
        low = (weight - high.astype(F32)).astype(BF16)
        both = jnp.concatenate([high, low], axis=0)
        parts = dot(both, right[...], ((1,), (0,)))
        query_grad = rounded(parts[0:block] + parts[block:])
        query_grads[rels, at, :] = query_grad.reshape(chunk_rels, share, width)
        twice = jnp.concatenate([query, query], axis=0)
        slab_grad = dot(twice, both, ((0,), (0,)))
        if chunk == 0:
            acc[bucket] = slab_grad
        else:
            acc[bucket] += slab_grad

    y_copies = []

    def send_pair(chunk):
        for rel in range(chunk * chunk_rels, (chunk + 1) * chunk_rels):
            outer = dot(lefts[rel].astype(BF16), query_grads[rel].astype(BF16), ((0,), (0,)))
            for level in range(levels):
                for side in range(2):
                    first = (level * 2 + side) * out_rows
                    rel_acc[side, level, rel * out_rows : (rel + 1) * out_rows, :] = outer[first : first + out_rows]
        rows = slice(chunk * chunk_rows, (chunk + 1) * chunk_rows)
        y_send[chunk] = rel_acc[1 - y, :, rows, :].astype(BF16)
        y_copies.append(
            send(y_send.at[chunk], y_recv.at[chunk], y_ss.at[chunk], y_rs.at[chunk], (dom + 1 - 2 * y, span))
        )

    z_copies = []

    def send_level(chunk):
        y_copies[chunk].wait()
        rows = slice(chunk * chunk_rows, (chunk + 1) * chunk_rows)
        total = rel_acc[y, :, rows, :] + y_recv[chunk].astype(F32)
        rel_acc[y, :, rows, :] = total
        z_send[chunk] = total.astype(BF16)
        for offset in range(1, levels):
            level = lax.rem(z + offset, levels)
            z_copies.append(
                send(
                    z_send.at[chunk, level],
                    z_recv.at[chunk, offset],
                    z_ss.at[chunk, offset],
                    z_rs.at[chunk, offset],
                    (level * 2 + y, span),
                )
            )

    def left_part(chunk):
        rels = range(chunk * chunk_rels, (chunk + 1) * chunk_rels)
        turned = [rounded(dot(query_grads[rel].astype(BF16), ops[rel], ((1,), (1,)))) for rel in rels]
        rows, marks = [], []
        for bucket in range(buckets):
            rows += [value[bucket * share : (bucket + 1) * share] for value in turned]
            marks.append(onehot[bucket, chunk * block : (chunk + 1) * block, :])
        rows = jnp.concatenate(rows, axis=0).astype(BF16)
        acc[0] += dot(rows, jnp.concatenate(marks, axis=0), ((0,), (0,)))

    def send_grads(bucket):
        total = jnp.transpose(acc[bucket])
        own_grad[bucket] = total
        for holder in range(groups):
            grad_send[bucket, holder] = total[holder * own_rows : (holder + 1) * own_rows].astype(BF16)
        copies = []
        for offset in range(1, groups):
            peer = span_peer(offset)
            copies.append(
                send(
                    grad_send.at[bucket, peer[1]],
                    grad_recv.at[bucket, offset],
                    grad_ss.at[bucket, offset],
                    grad_rs.at[bucket, offset],
                    peer,
                )
            )
        return copies

    def gathered(bucket, copies):
        for copy in copies:
            copy.wait()
        total = own_grad[bucket, pl.ds(pl.multiple_of(span * own_rows, own_rows), own_rows), :]
        for offset in range(1, groups):
            total = total + grad_recv[bucket, offset].astype(F32)
        return total

    for chunk in range(chunks):
        score(chunk, 0)
    for copy in slab_copies:
        copy.wait()
    for chunk in range(chunks):
        for bucket in range(1, buckets):
            score(chunk, bucket)
        send_pair(chunk)
        if chunk > 0:
            send_level(chunk - 1)
        if chunk < chunks - 1:
            left_part(chunk)
    grad_copies = [None] + [send_grads(bucket) for bucket in range(1, buckets)]
    left_part(chunks - 1)
    grad_copies[0] = send_grads(0)
    send_level(chunks - 1)

    home_copies = []
    for bucket in range(1, buckets):
        home_send[bucket] = gathered(bucket, grad_copies[bucket]).astype(BF16)
        home_copies.append(
            send(home_send.at[bucket], home_recv.at[bucket], home_ss.at[bucket], home_rs.at[bucket], dom_peer(bucket))
        )
    total = gathered(0, grad_copies[0])
    for bucket in range(1, buckets):
        home_copies[bucket - 1].wait()
        total = total + home_recv[bucket].astype(F32)
    ent_out[...] = total

    for chunk in range(chunks):
        for copy in z_copies[chunk * (levels - 1) : (chunk + 1) * (levels - 1)]:
            copy.wait()
        rows = slice(chunk * chunk_rows, (chunk + 1) * chunk_rows)
        total = rel_acc[y, z, rows, :]
        for offset in range(1, levels):
            total = total + z_recv[chunk, offset].astype(F32)
        rel_out[rows, :] = total


def hand_over(ent_grad, rel_grad, ent_out, rel_out):
    ent_out[...] = ent_grad[...]
    rel_out[...] = rel_grad[...]


def shards(entities, operators, left_rows, right_rows, negatives, counts):
    buckets = left_rows.shape[0]
    slot_count = left_rows.shape[-1]
    neg_count = negatives.shape[-1]
    groups = lax.axis_size("span")
    doms = lax.axis_size("dom")
    rel_own = operators.shape[0]
    cap = slot_count // (rel_own * groups)
    slots = rel_own * cap
    part_rows, width = entities.shape
    own_rows = part_rows // groups
    out_rows = width // doms
    levels = doms // 2
    chunks = 4 if (rel_own // 4) * out_rows % 16 == 0 else 2
    chunk_rows = rel_own // chunks * out_rows
    mult_rows = part_rows // LANES
    meta_rows = MULT_AT + -(-buckets * mult_rows // 8) * 8
    edges = buckets * groups * cap
    dims = (buckets, doms, groups, rel_own, cap, chunks)
    dma = pltpu.SemaphoreType.DMA
    vmem = pl.BlockSpec(memory_space=pltpu.VMEM)
    ent_grad, rel_grad = pl.pallas_call(
        functools.partial(kernel, dims),
        out_shape=(
            jax.ShapeDtypeStruct((own_rows, width), F32),
            jax.ShapeDtypeStruct((rel_own * out_rows, width), F32),
        ),
        in_specs=[vmem] * 6,
        out_specs=(vmem, vmem),
        scratch_shapes=[
            pltpu.VMEM((buckets - 1, part_rows, width), BF16),
            pltpu.VMEM((groups, meta_rows, LANES), F32),
            pltpu.VMEM((groups, meta_rows, LANES), F32),
            pltpu.VMEM((rel_own, groups * cap, MULT_AT), F32),
            pltpu.VMEM((buckets, groups * cap, part_rows), F32),
            pltpu.VMEM((buckets, groups * slots, part_rows), BF16),
            pltpu.VMEM((rel_own, edges, width), F32),
            pltpu.VMEM((rel_own, edges, width), F32),
            pltpu.VMEM((rel_own, edges, width), F32),
            pltpu.VMEM((buckets, width, part_rows), F32),
            pltpu.VMEM((buckets, part_rows, width), F32),
            pltpu.VMEM((buckets, groups, own_rows, width), BF16),
            pltpu.VMEM((buckets, groups, own_rows, width), BF16),
            pltpu.VMEM((buckets, own_rows, width), BF16),
            pltpu.VMEM((buckets, own_rows, width), BF16),
            pltpu.VMEM((2, levels, rel_own * out_rows, width), F32),
            pltpu.VMEM((chunks, levels, chunk_rows, width), BF16),
            pltpu.VMEM((chunks, levels, chunk_rows, width), BF16),
            pltpu.VMEM((chunks, levels, chunk_rows, width), BF16),
            pltpu.VMEM((chunks, levels, chunk_rows, width), BF16),
            dma((groups,)),
            dma((groups,)),
            dma((buckets - 1, groups)),
            dma((buckets - 1, groups)),
            dma((buckets, groups)),
            dma((buckets, groups)),
            dma((buckets,)),
            dma((buckets,)),
            dma((chunks,)),
            dma((chunks,)),
            dma((chunks, levels)),
            dma((chunks, levels)),
        ],
        compiler_params=pltpu.CompilerParams(
            collective_id=0, has_side_effects=True, vmem_limit_bytes=58 * 1024 * 1024
        ),
        name="train_step",
    )(entities, operators, left_rows, right_rows, negatives, counts)
    ent_grad, rel_grad = pl.pallas_call(
        hand_over,
        out_shape=(
            jax.ShapeDtypeStruct(ent_grad.shape, F32),
            jax.ShapeDtypeStruct(rel_grad.shape, F32),
        ),
        in_specs=[vmem] * 2,
        out_specs=(vmem, vmem),
        name="hand_over",
    )(ent_grad, rel_grad)
    return (ent_grad, rel_grad.reshape(rel_own, out_rows, width))


def solution(mesh):
    in_specs = (
        P("dom", None),
        P("span", None, None),
        P(None, "dom", "span", None),
        P(None, "dom", "span", None),
        P(None, "dom", "span", None),
        P(None, "dom", "span", None),
    )
    out_specs = (P(("dom", "span"), None), P("span", "dom", None))
    return jax.shard_map(shards, mesh=mesh, in_specs=in_specs, out_specs=out_specs, check_vma=False)
```

```python
import functools

import jax
import jax.numpy as jnp
from jax import lax
from jax.experimental import pallas as pl
from jax.experimental.pallas import tpu as pltpu
from jax.sharding import PartitionSpec as P

MESH = pl.DeviceIdType.MESH
F32 = jnp.float32
BF16 = jnp.bfloat16
LANES = 128
MULT_AT = 16


def dot(a, b, dims):
    return lax.dot_general(a, b, (dims, ((), ())), preferred_element_type=F32)


def rounded(value):
    return value.astype(BF16).astype(F32)


def kernel(
    dims,
    ent,
    ops,
    left_rows,
    right_rows,
    negatives,
    counts,
    ent_out,
    rel_out,
    slabs,
    meta_send,
    meta,
    cols,
    times,
    onehot,
    lefts,
    queries,
    query_grads,
    acc,
    own_grad,
    pair_recv,
    grad_send,
    grad_recv,
    home_send,
    home_recv,
    rel_acc,
    y_send,
    y_recv,
    z_send,
    z_recv,
    meta_ss,
    meta_rs,
    slab_ss,
    slab_rs,
    pair_ss,
    pair_rs,
    grad_ss,
    grad_rs,
    home_ss,
    home_rs,
    y_ss,
    y_rs,
    z_ss,
    z_rs,
):
    buckets, doms, groups, rel_own, cap, chunks, pieces = dims
    part_rows, width = ent.shape
    slot_count = left_rows.shape[-1]
    neg_count = negatives.shape[-1]
    relations = rel_own * groups
    slots = rel_own * cap
    levels = doms // 2
    own_rows = part_rows // groups
    out_rows = width // doms
    chunk_rels = rel_own // chunks
    piece_rels = chunk_rels // pieces
    piece_rows = piece_rels * out_rows
    half = groups // 2
    share = groups * cap
    block = chunk_rels * share
    mult_rows = part_rows // LANES
    neg_scale = float(neg_count) ** (-0.5)
    dom = lax.axis_index("dom")
    span = lax.axis_index("span")
    y = lax.rem(dom, 2)
    z = lax.div(dom, 2)
    core = lax.rem(span, 2)
    chip = lax.div(span, 2)

    def span_peer(offset):
        return (dom, lax.rem(span + offset, groups))

    def dom_peer(offset):
        return (lax.rem(dom + offset + doms, doms), span)

    def send(src, dst, send_sem, recv_sem, peer):
        copy = pltpu.make_async_remote_copy(
            src_ref=src,
            dst_ref=dst,
            send_sem=send_sem,
            recv_sem=recv_sem,
            device_id=peer,
            device_id_type=MESH,
        )
        copy.start()
        return copy

    barrier = pltpu.get_barrier_semaphore()
    for offset in range(1, groups):
        pl.semaphore_signal(barrier, inc=1, device_id=span_peer(offset), device_id_type=MESH)
    for offset in range(1, doms):
        pl.semaphore_signal(barrier, inc=1, device_id=dom_peer(offset), device_id_type=MESH)

    def rows_of(ref):
        return jnp.concatenate([ref[bucket, 0] for bucket in range(buckets)], axis=0)

    expand = (
        lax.broadcasted_iota(jnp.int32, (relations, slot_count), 1) // cap
        == lax.broadcasted_iota(jnp.int32, (relations, slot_count), 0)
    )
    wide_counts = dot(
        rows_of(counts).astype(F32).astype(BF16),
        jnp.where(expand, 1.0, 0.0).astype(BF16),
        ((1,), (0,)),
    )
    place = (lax.broadcasted_iota(jnp.int32, (buckets, slot_count), 1) % cap).astype(F32)
    live = jnp.where(wide_counts > place, 1.0, 0.0)
    left_wide = rows_of(left_rows).astype(F32)
    right_wide = rows_of(right_rows).astype(F32)
    meta_send[...] = jnp.zeros(meta_send.shape, F32)
    for holder in range(groups):
        cut = slice(holder * slots, (holder + 1) * slots)
        meta_send[holder, 0:buckets, 0:slots] = left_wide[:, cut]
        meta_send[holder, buckets : 2 * buckets, 0:slots] = right_wide[:, cut]
        meta_send[holder, 2 * buckets : 3 * buckets, 0:slots] = live[:, cut]
    for bucket in range(buckets):
        row = negatives[bucket, 0]
        high = lax.broadcasted_iota(jnp.int32, (mult_rows, neg_count), 0) == row // LANES
        low = lax.broadcasted_iota(jnp.int32, (LANES, neg_count), 0) == row % LANES
        mult = dot(
            jnp.where(high, 1.0, 0.0).astype(BF16),
            jnp.where(low, 1.0, 0.0).astype(BF16),
            ((1,), (1,)),
        )
        at = MULT_AT + bucket * mult_rows
        for holder in range(groups):
            meta_send[holder, at : at + mult_rows, :] = mult

    pl.semaphore_wait(barrier, groups - 1 + doms - 1)
    meta_copies = []
    for offset in range(1, groups):
        peer = span_peer(offset)
        meta_copies.append(
            send(meta_send.at[peer[1]], meta.at[offset], meta_ss.at[offset], meta_rs.at[offset], peer)
        )
    part = pl.ds(pl.multiple_of(span * own_rows, own_rows), own_rows)
    slab_parts = [
        send(ent.at[part], slabs.at[b - 1, part], slab_ss.at[b - 1, 0], slab_rs.at[b - 1, 0], dom_peer(-b))
        for b in range(1, buckets)
    ]
    meta[0] = meta_send[span]
    for copy in meta_copies:
        copy.wait()

    lane_row = lax.broadcasted_iota(jnp.int32, (block, part_rows), 1).astype(F32)
    for group in range(groups):
        turned = jnp.transpose(meta[group, 0:MULT_AT, :])
        cols[:, group * cap : (group + 1) * cap, :] = turned[0:slots].reshape(rel_own, cap, MULT_AT)
        for bucket in range(buckets):
            first = MULT_AT + bucket * mult_rows
            mult = jnp.concatenate(
                [meta[group, first + part : first + part + 1, :] for part in range(mult_rows)], axis=1
            )
            times[bucket, group * cap : (group + 1) * cap, :] = jnp.broadcast_to(mult, (cap, part_rows))

    def column(chunk, which):
        held = cols[chunk * chunk_rels : (chunk + 1) * chunk_rels].reshape(block, MULT_AT)
        return held[:, which : which + 1]

    for bucket in range(buckets):
        for chunk in range(chunks):
            hit = lane_row == column(chunk, bucket)
            onehot[bucket, chunk * block : (chunk + 1) * block, :] = jnp.where(hit, 1.0, 0.0).astype(BF16)
        picked = dot(onehot[bucket], ent[...], ((1,), (0,)))
        lefts[:, bucket * share : (bucket + 1) * share, :] = picked.reshape(rel_own, share, width)
    slab_copies = []
    for b in range(1, buckets):
        slab_parts[b - 1].wait()
        slab_copies.append([])
        for offset in range(1, groups):
            slab_copies[b - 1].append(
                send(
                    slabs.at[b - 1, part],
                    slabs.at[b - 1, part],
                    slab_ss.at[b - 1, offset],
                    slab_rs.at[b - 1, offset],
                    span_peer(offset),
                )
            )
    for rel in range(rel_own):
        queries[rel] = rounded(dot(lefts[rel].astype(BF16), ops[rel], ((1,), (0,))))

    def score(chunk, bucket):
        right = ent if bucket == 0 else slabs.at[bucket - 1]
        rels = slice(chunk * chunk_rels, (chunk + 1) * chunk_rels)
        at = slice(bucket * share, (bucket + 1) * share)
        query = queries[rels, at, :].reshape(block, width).astype(BF16)
        live_col = column(chunk, 2 * buckets + bucket)
        scores = dot(query, right[...], ((1,), (1,)))
        hit = lane_row == column(chunk, buckets + bucket)
        positive = jnp.sum(jnp.where(hit, scores, 0.0), axis=1, keepdims=True)
        pos_grad = -live_col * jax.nn.sigmoid(-positive)
        neg_grad = rounded((jnp.tanh(scores * 0.5) + 1.0) * (live_col * (0.5 * neg_scale)))
        counted = neg_grad.reshape(chunk_rels, share, part_rows) * times[bucket][None]
        weight = counted.reshape(block, part_rows) + jnp.where(hit, pos_grad, 0.0)
        high = weight.astype(BF16)
        low = (weight - high.astype(F32)).astype(BF16)
        both = jnp.concatenate([high, low], axis=0)
        parts = dot(both, right[...], ((1,), (0,)))
        query_grad = rounded(parts[0:block] + parts[block:])
        query_grads[rels, at, :] = query_grad.reshape(chunk_rels, share, width)
        twice = jnp.concatenate([query, query], axis=0)
        slab_grad = dot(twice, both, ((0,), (0,)))
        if chunk == 0:
            acc[bucket] = slab_grad
        else:
            acc[bucket] += slab_grad

    y_copies = []

    def send_pair(piece):
        for rel in range(piece * piece_rels, (piece + 1) * piece_rels):
            outer = dot(lefts[rel].astype(BF16), query_grads[rel].astype(BF16), ((0,), (0,)))
            for level in range(levels):
                for side in range(2):
                    first = (level * 2 + side) * out_rows
                    rel_acc[side, level, rel * out_rows : (rel + 1) * out_rows, :] = outer[first : first + out_rows]
        rows = slice(piece * piece_rows, (piece + 1) * piece_rows)
        y_send[piece] = rel_acc[1 - y, :, rows, :].astype(BF16)
        y_copies.append(
            send(y_send.at[piece], y_recv.at[piece], y_ss.at[piece], y_rs.at[piece], (dom + 1 - 2 * y, span))
        )

    z_copies = []

    def send_level(piece):
        y_copies[piece].wait()
        rows = slice(piece * piece_rows, (piece + 1) * piece_rows)
        total = rel_acc[y, :, rows, :] + y_recv[piece].astype(F32)
        rel_acc[y, :, rows, :] = total
        z_send[piece] = total.astype(BF16)
        for offset in range(1, levels):
            level = lax.rem(z + offset, levels)
            z_copies.append(
                send(
                    z_send.at[piece, level],
                    z_recv.at[piece, offset],
                    z_ss.at[piece, offset],
                    z_rs.at[piece, offset],
                    (level * 2 + y, span),
                )
            )

    def left_part(chunk):
        rels = range(chunk * chunk_rels, (chunk + 1) * chunk_rels)
        turned = [rounded(dot(query_grads[rel].astype(BF16), ops[rel], ((1,), (1,)))) for rel in rels]
        rows, marks = [], []
        for bucket in range(buckets):
            rows += [value[bucket * share : (bucket + 1) * share] for value in turned]
            marks.append(onehot[bucket, chunk * block : (chunk + 1) * block, :])
        rows = jnp.concatenate(rows, axis=0).astype(BF16)
        acc[0] += dot(rows, jnp.concatenate(marks, axis=0), ((0,), (0,)))

    pair_copies = {}
    chip_copies = {}
    home_copies = {}

    def send_core(bucket):
        total = jnp.transpose(acc[bucket])
        for holder in range(groups):
            own_grad[bucket, holder % 2, holder // 2] = total[holder * own_rows : (holder + 1) * own_rows]
        pair_copies[bucket] = send(
            own_grad.at[bucket, 1 - core],
            pair_recv.at[bucket],
            pair_ss.at[bucket],
            pair_rs.at[bucket],
            (dom, span + 1 - 2 * core),
        )

    def send_chip(bucket):
        pair_copies[bucket].wait()
        total = own_grad[bucket, core] + pair_recv[bucket]
        own_grad[bucket, core] = total
        grad_send[bucket] = total.astype(BF16)
        chip_copies[bucket] = []
        for offset in range(1, half):
            to_chip = lax.rem(chip + offset, half)
            chip_copies[bucket].append(
                send(
                    grad_send.at[bucket, to_chip],
                    grad_recv.at[bucket, offset],
                    grad_ss.at[bucket, offset],
                    grad_rs.at[bucket, offset],
                    (dom, to_chip * 2 + core),
                )
            )

    def gathered(bucket):
        for copy in chip_copies[bucket]:
            copy.wait()
        total = own_grad[bucket, core, chip]
        for offset in range(1, half):
            total = total + grad_recv[bucket, offset].astype(F32)
        return total

    def send_home(bucket):
        home_send[bucket] = gathered(bucket).astype(BF16)
        home_copies[bucket] = send(
            home_send.at[bucket], home_recv.at[bucket], home_ss.at[bucket], home_rs.at[bucket], dom_peer(bucket)
        )

    last = chunks - 1
    for chunk in range(chunks):
        score(chunk, 0)
    for chunk in range(chunks):
        for bucket in range(1, buckets):
            if chunk == 0:
                for copy in slab_copies[bucket - 1]:
                    copy.wait()
            score(chunk, bucket)
            if chunk == last and bucket < buckets - 1:
                send_core(bucket)
        for piece in range(chunk * pieces, (chunk + 1) * pieces):
            send_pair(piece)
        if chunk == last:
            send_core(buckets - 1)
        if chunk > 0:
            for piece in range((chunk - 1) * pieces, chunk * pieces):
                send_level(piece)
        if chunk < last:
            left_part(chunk)
    for bucket in range(1, buckets):
        send_chip(bucket)
    left_part(last)
    send_core(0)
    for bucket in range(1, buckets):
        send_home(bucket)
    for piece in range(last * pieces, chunks * pieces):
        send_level(piece)
    send_chip(0)
    total = gathered(0)
    for bucket in range(1, buckets):
        home_copies[bucket].wait()
        total = total + home_recv[bucket].astype(F32)
    ent_out[...] = total

    for piece in range(chunks * pieces):
        for copy in z_copies[piece * (levels - 1) : (piece + 1) * (levels - 1)]:
            copy.wait()
        rows = slice(piece * piece_rows, (piece + 1) * piece_rows)
        total = rel_acc[y, z, rows, :]
        for offset in range(1, levels):
            total = total + z_recv[piece, offset].astype(F32)
        rel_out[rows, :] = total


def hand_over(ent_grad, rel_grad, ent_out, rel_out):
    ent_out[...] = ent_grad[...]
    rel_out[...] = rel_grad[...]


def shards(entities, operators, left_rows, right_rows, negatives, counts):
    buckets = left_rows.shape[0]
    slot_count = left_rows.shape[-1]
    neg_count = negatives.shape[-1]
    groups = lax.axis_size("span")
    doms = lax.axis_size("dom")
    rel_own = operators.shape[0]
    cap = slot_count // (rel_own * groups)
    slots = rel_own * cap
    part_rows, width = entities.shape
    own_rows = part_rows // groups
    out_rows = width // doms
    levels = doms // 2
    chunks = 4 if (rel_own // 4) * out_rows % 16 == 0 else 2
    pieces = 2 if (rel_own // chunks // 2) * out_rows % 16 == 0 else 1
    piece_rows = rel_own // chunks // pieces * out_rows
    half = groups // 2
    mult_rows = part_rows // LANES
    meta_rows = MULT_AT + -(-buckets * mult_rows // 8) * 8
    edges = buckets * groups * cap
    dims = (buckets, doms, groups, rel_own, cap, chunks, pieces)
    dma = pltpu.SemaphoreType.DMA
    vmem = pl.BlockSpec(memory_space=pltpu.VMEM)
    ent_grad, rel_grad = pl.pallas_call(
        functools.partial(kernel, dims),
        out_shape=(
            jax.ShapeDtypeStruct((own_rows, width), F32),
            jax.ShapeDtypeStruct((rel_own * out_rows, width), F32),
        ),
        in_specs=[vmem] * 6,
        out_specs=(vmem, vmem),
        scratch_shapes=[
            pltpu.VMEM((buckets - 1, part_rows, width), BF16),
            pltpu.VMEM((groups, meta_rows, LANES), F32),
            pltpu.VMEM((groups, meta_rows, LANES), F32),
            pltpu.VMEM((rel_own, groups * cap, MULT_AT), F32),
            pltpu.VMEM((buckets, groups * cap, part_rows), F32),
            pltpu.VMEM((buckets, groups * slots, part_rows), BF16),
            pltpu.VMEM((rel_own, edges, width), F32),
            pltpu.VMEM((rel_own, edges, width), F32),
            pltpu.VMEM((rel_own, edges, width), F32),
            pltpu.VMEM((buckets, width, part_rows), F32),
            pltpu.VMEM((buckets, 2, half, own_rows, width), F32),
            pltpu.VMEM((buckets, half, own_rows, width), F32),
            pltpu.VMEM((buckets, half, own_rows, width), BF16),
            pltpu.VMEM((buckets, half, own_rows, width), BF16),
            pltpu.VMEM((buckets, own_rows, width), BF16),
            pltpu.VMEM((buckets, own_rows, width), BF16),
            pltpu.VMEM((2, levels, rel_own * out_rows, width), F32),
            pltpu.VMEM((chunks * pieces, levels, piece_rows, width), BF16),
            pltpu.VMEM((chunks * pieces, levels, piece_rows, width), BF16),
            pltpu.VMEM((chunks * pieces, levels, piece_rows, width), BF16),
            pltpu.VMEM((chunks * pieces, levels, piece_rows, width), BF16),
            dma((groups,)),
            dma((groups,)),
            dma((buckets - 1, groups)),
            dma((buckets - 1, groups)),
            dma((buckets,)),
            dma((buckets,)),
            dma((buckets, half)),
            dma((buckets, half)),
            dma((buckets,)),
            dma((buckets,)),
            dma((chunks * pieces,)),
            dma((chunks * pieces,)),
            dma((chunks * pieces, levels)),
            dma((chunks * pieces, levels)),
        ],
        compiler_params=pltpu.CompilerParams(
            collective_id=0, has_side_effects=True, vmem_limit_bytes=58 * 1024 * 1024
        ),
        name="train_step",
    )(entities, operators, left_rows, right_rows, negatives, counts)
    ent_grad, rel_grad = pl.pallas_call(
        hand_over,
        out_shape=(
            jax.ShapeDtypeStruct(ent_grad.shape, F32),
            jax.ShapeDtypeStruct(rel_grad.shape, F32),
        ),
        in_specs=[vmem] * 2,
        out_specs=(vmem, vmem),
        name="hand_over",
    )(ent_grad, rel_grad)
    return (ent_grad, rel_grad.reshape(rel_own, out_rows, width))


def solution(mesh):
    in_specs = (
        P("dom", None),
        P("span", None, None),
        P(None, "dom", "span", None),
        P(None, "dom", "span", None),
        P(None, "dom", "span", None),
        P(None, "dom", "span", None),
    )
    out_specs = (P(("dom", "span"), None), P("span", "dom", None))
    return jax.shard_map(shards, mesh=mesh, in_specs=in_specs, out_specs=out_specs, check_vma=False)
```

```python
import functools

import jax
import jax.numpy as jnp
from jax import lax
from jax.experimental import pallas as pl
from jax.experimental.pallas import tpu as pltpu
from jax.sharding import PartitionSpec as P

MESH = pl.DeviceIdType.MESH
F32 = jnp.float32
BF16 = jnp.bfloat16
LANES = 128
MULT_AT = 16


def dot(a, b, dims):
    return lax.dot_general(a, b, (dims, ((), ())), preferred_element_type=F32)


def rounded(value):
    return value.astype(BF16).astype(F32)


def kernel(
    dims,
    ent,
    ops,
    left_rows,
    right_rows,
    negatives,
    counts,
    ent_out,
    rel_out,
    slabs,
    meta_send,
    meta,
    cols,
    times,
    onehot,
    lefts,
    queries,
    query_grads,
    acc,
    own_grad,
    pair_recv,
    grad_send,
    grad_recv,
    home_send,
    home_recv,
    rel_acc,
    y_send,
    y_recv,
    z_send,
    z_recv,
    meta_ss,
    meta_rs,
    slab_ss,
    slab_rs,
    pair_ss,
    pair_rs,
    grad_ss,
    grad_rs,
    home_ss,
    home_rs,
    y_ss,
    y_rs,
    z_ss,
    z_rs,
):
    buckets, doms, groups, rel_own, cap, chunks, pieces = dims
    part_rows, width = ent.shape
    slot_count = left_rows.shape[-1]
    neg_count = negatives.shape[-1]
    relations = rel_own * groups
    slots = rel_own * cap
    levels = doms // 2
    own_rows = part_rows // groups
    out_rows = width // doms
    chunk_rels = rel_own // chunks
    piece_rels = chunk_rels // pieces
    piece_rows = piece_rels * out_rows
    half = groups // 2
    share = groups * cap
    block = chunk_rels * share
    mult_rows = part_rows // LANES
    neg_scale = float(neg_count) ** (-0.5)
    dom = lax.axis_index("dom")
    span = lax.axis_index("span")
    y = lax.rem(dom, 2)
    z = lax.div(dom, 2)
    core = lax.rem(span, 2)
    chip = lax.div(span, 2)

    def span_peer(offset):
        return (dom, lax.rem(span + offset, groups))

    def dom_peer(offset):
        return (lax.rem(dom + offset + doms, doms), span)

    def send(src, dst, send_sem, recv_sem, peer):
        copy = pltpu.make_async_remote_copy(
            src_ref=src,
            dst_ref=dst,
            send_sem=send_sem,
            recv_sem=recv_sem,
            device_id=peer,
            device_id_type=MESH,
        )
        copy.start()
        return copy

    barrier = pltpu.get_barrier_semaphore()
    for offset in range(1, groups):
        pl.semaphore_signal(barrier, inc=1, device_id=span_peer(offset), device_id_type=MESH)
    for offset in range(1, doms):
        pl.semaphore_signal(barrier, inc=1, device_id=dom_peer(offset), device_id_type=MESH)

    def rows_of(ref):
        return jnp.concatenate([ref[bucket, 0] for bucket in range(buckets)], axis=0)

    expand = (
        lax.broadcasted_iota(jnp.int32, (relations, slot_count), 1) // cap
        == lax.broadcasted_iota(jnp.int32, (relations, slot_count), 0)
    )
    wide_counts = dot(
        rows_of(counts).astype(F32).astype(BF16),
        jnp.where(expand, 1.0, 0.0).astype(BF16),
        ((1,), (0,)),
    )
    place = (lax.broadcasted_iota(jnp.int32, (buckets, slot_count), 1) % cap).astype(F32)
    live = jnp.where(wide_counts > place, 1.0, 0.0)
    left_wide = rows_of(left_rows).astype(F32)
    right_wide = rows_of(right_rows).astype(F32)
    meta_send[...] = jnp.zeros(meta_send.shape, F32)
    for holder in range(groups):
        cut = slice(holder * slots, (holder + 1) * slots)
        meta_send[holder, 0:buckets, 0:slots] = left_wide[:, cut]
        meta_send[holder, buckets : 2 * buckets, 0:slots] = right_wide[:, cut]
        meta_send[holder, 2 * buckets : 3 * buckets, 0:slots] = live[:, cut]
    for bucket in range(buckets):
        row = negatives[bucket, 0]
        high = lax.broadcasted_iota(jnp.int32, (mult_rows, neg_count), 0) == row // LANES
        low = lax.broadcasted_iota(jnp.int32, (LANES, neg_count), 0) == row % LANES
        mult = dot(
            jnp.where(high, 1.0, 0.0).astype(BF16),
            jnp.where(low, 1.0, 0.0).astype(BF16),
            ((1,), (1,)),
        )
        at = MULT_AT + bucket * mult_rows
        for holder in range(groups):
            meta_send[holder, at : at + mult_rows, :] = mult

    pl.semaphore_wait(barrier, groups - 1 + doms - 1)
    meta_copies = []
    for offset in range(1, groups):
        peer = span_peer(offset)
        meta_copies.append(
            send(meta_send.at[peer[1]], meta.at[offset], meta_ss.at[offset], meta_rs.at[offset], peer)
        )
    part = pl.ds(pl.multiple_of(span * own_rows, own_rows), own_rows)
    slab_parts = [
        send(ent.at[part], slabs.at[b - 1, part], slab_ss.at[b - 1, 0], slab_rs.at[b - 1, 0], dom_peer(-b))
        for b in range(1, buckets)
    ]
    meta[0] = meta_send[span]
    for copy in meta_copies:
        copy.wait()

    lane_row = lax.broadcasted_iota(jnp.int32, (block, part_rows), 1).astype(F32)
    for group in range(groups):
        turned = jnp.transpose(meta[group, 0:MULT_AT, :])
        cols[:, group * cap : (group + 1) * cap, :] = turned[0:slots].reshape(rel_own, cap, MULT_AT)
        for bucket in range(buckets):
            first = MULT_AT + bucket * mult_rows
            mult = jnp.concatenate(
                [meta[group, first + part : first + part + 1, :] for part in range(mult_rows)], axis=1
            )
            times[bucket, group * cap : (group + 1) * cap, :] = jnp.broadcast_to(mult, (cap, part_rows))

    def column(chunk, which, wide=1):
        held = cols[chunk * chunk_rels : (chunk + wide) * chunk_rels].reshape(wide * block, MULT_AT)
        return held[:, which : which + 1]

    for bucket in range(buckets):
        for chunk in range(chunks):
            hit = lane_row == column(chunk, bucket)
            onehot[bucket, chunk * block : (chunk + 1) * block, :] = jnp.where(hit, 1.0, 0.0).astype(BF16)
        picked = dot(onehot[bucket], ent[...], ((1,), (0,)))
        lefts[:, bucket * share : (bucket + 1) * share, :] = picked.reshape(rel_own, share, width)
    slab_copies = []

    def pass_on(b):
        slab_parts[b - 1].wait()
        slab_copies.append([])
        for offset in range(1, groups):
            slab_copies[b - 1].append(
                send(
                    slabs.at[b - 1, part],
                    slabs.at[b - 1, part],
                    slab_ss.at[b - 1, offset],
                    slab_rs.at[b - 1, offset],
                    span_peer(offset),
                )
            )

    for rel in range(rel_own):
        queries[rel] = rounded(dot(lefts[rel].astype(BF16), ops[rel], ((1,), (0,))))

    def score(chunk, bucket, wide=1):
        edges = wide * block
        many = wide * chunk_rels
        lane_row = lax.broadcasted_iota(jnp.int32, (edges, part_rows), 1).astype(F32)
        right = ent if bucket == 0 else slabs.at[bucket - 1]
        rels = slice(chunk * chunk_rels, (chunk + wide) * chunk_rels)
        at = slice(bucket * share, (bucket + 1) * share)
        query = queries[rels, at, :].reshape(edges, width).astype(BF16)
        live_col = column(chunk, 2 * buckets + bucket, wide)
        scores = dot(query, right[...], ((1,), (1,)))
        hit = lane_row == column(chunk, buckets + bucket, wide)
        positive = jnp.sum(jnp.where(hit, scores, 0.0), axis=1, keepdims=True)
        pos_grad = -live_col * jax.nn.sigmoid(-positive)
        neg_grad = rounded((jnp.tanh(scores * 0.5) + 1.0) * (live_col * (0.5 * neg_scale)))
        counted = neg_grad.reshape(many, share, part_rows) * times[bucket][None]
        weight = counted.reshape(edges, part_rows) + jnp.where(hit, pos_grad, 0.0)
        high = weight.astype(BF16)
        low = (weight - high.astype(F32)).astype(BF16)
        both = jnp.concatenate([high, low], axis=0)
        parts = dot(both, right[...], ((1,), (0,)))
        query_grad = rounded(parts[0:edges] + parts[edges:])
        query_grads[rels, at, :] = query_grad.reshape(many, share, width)
        twice = jnp.concatenate([query, query], axis=0)
        slab_grad = dot(twice, both, ((0,), (0,)))
        if chunk == 0:
            acc[bucket] = slab_grad
        else:
            acc[bucket] += slab_grad

    y_copies = []

    def send_pair(piece):
        for rel in range(piece * piece_rels, (piece + 1) * piece_rels):
            outer = dot(lefts[rel].astype(BF16), query_grads[rel].astype(BF16), ((0,), (0,)))
            for level in range(levels):
                for side in range(2):
                    first = (level * 2 + side) * out_rows
                    rel_acc[side, level, rel * out_rows : (rel + 1) * out_rows, :] = outer[first : first + out_rows]
        rows = slice(piece * piece_rows, (piece + 1) * piece_rows)
        y_send[piece] = rel_acc[1 - y, :, rows, :].astype(BF16)
        y_copies.append(
            send(y_send.at[piece], y_recv.at[piece], y_ss.at[piece], y_rs.at[piece], (dom + 1 - 2 * y, span))
        )

    z_copies = []

    def send_level(piece):
        y_copies[piece].wait()
        rows = slice(piece * piece_rows, (piece + 1) * piece_rows)
        total = rel_acc[y, :, rows, :] + y_recv[piece].astype(F32)
        rel_acc[y, :, rows, :] = total
        z_send[piece] = total.astype(BF16)
        for offset in range(1, levels):
            level = lax.rem(z + offset, levels)
            z_copies.append(
                send(
                    z_send.at[piece, level],
                    z_recv.at[piece, offset],
                    z_ss.at[piece, offset],
                    z_rs.at[piece, offset],
                    (level * 2 + y, span),
                )
            )

    def left_part(chunk):
        rels = range(chunk * chunk_rels, (chunk + 1) * chunk_rels)
        turned = [rounded(dot(query_grads[rel].astype(BF16), ops[rel], ((1,), (1,)))) for rel in rels]
        rows, marks = [], []
        for bucket in range(buckets):
            rows += [value[bucket * share : (bucket + 1) * share] for value in turned]
            marks.append(onehot[bucket, chunk * block : (chunk + 1) * block, :])
        rows = jnp.concatenate(rows, axis=0).astype(BF16)
        acc[0] += dot(rows, jnp.concatenate(marks, axis=0), ((0,), (0,)))

    pair_copies = {}
    chip_copies = {}
    home_copies = {}

    def send_core(bucket):
        total = jnp.transpose(acc[bucket])
        for holder in range(groups):
            own_grad[bucket, holder % 2, holder // 2] = total[holder * own_rows : (holder + 1) * own_rows]
        pair_copies[bucket] = send(
            own_grad.at[bucket, 1 - core],
            pair_recv.at[bucket],
            pair_ss.at[bucket],
            pair_rs.at[bucket],
            (dom, span + 1 - 2 * core),
        )

    def send_chip(bucket):
        pair_copies[bucket].wait()
        total = own_grad[bucket, core] + pair_recv[bucket]
        own_grad[bucket, core] = total
        grad_send[bucket] = total.astype(BF16)
        chip_copies[bucket] = []
        for offset in range(1, half):
            to_chip = lax.rem(chip + offset, half)
            chip_copies[bucket].append(
                send(
                    grad_send.at[bucket, to_chip],
                    grad_recv.at[bucket, offset],
                    grad_ss.at[bucket, offset],
                    grad_rs.at[bucket, offset],
                    (dom, to_chip * 2 + core),
                )
            )

    def gathered(bucket):
        for copy in chip_copies[bucket]:
            copy.wait()
        total = own_grad[bucket, core, chip]
        for offset in range(1, half):
            total = total + grad_recv[bucket, offset].astype(F32)
        return total

    def send_home(bucket):
        home_send[bucket] = gathered(bucket).astype(BF16)
        home_copies[bucket] = send(
            home_send.at[bucket], home_recv.at[bucket], home_ss.at[bucket], home_rs.at[bucket], dom_peer(bucket)
        )

    last = chunks - 1
    pass_on(1)
    for chunk in range(0, chunks, 2):
        score(chunk, 0, 2)
        if chunk == 0:
            for bucket in range(2, buckets):
                pass_on(bucket)
    for chunk in range(chunks):
        for bucket in range(1, buckets):
            if chunk == 0:
                for copy in slab_copies[bucket - 1]:
                    copy.wait()
            if bucket == buckets - 1:
                score(chunk, bucket)
            elif chunk % 2 == 0:
                score(chunk, bucket, 2)
                if chunk == last - 1:
                    send_core(bucket)
        for piece in range(chunk * pieces, (chunk + 1) * pieces):
            send_pair(piece)
        if chunk == last:
            send_core(buckets - 1)
        if chunk > 0:
            for piece in range((chunk - 1) * pieces, chunk * pieces):
                send_level(piece)
        if chunk < last:
            left_part(chunk)
    for bucket in range(1, buckets):
        send_chip(bucket)
    left_part(last)
    send_core(0)
    for bucket in range(1, buckets):
        send_home(bucket)
    for piece in range(last * pieces, chunks * pieces):
        send_level(piece)
    send_chip(0)
    total = gathered(0)
    for bucket in range(1, buckets):
        home_copies[bucket].wait()
        total = total + home_recv[bucket].astype(F32)
    ent_out[...] = total

    for piece in range(chunks * pieces):
        for copy in z_copies[piece * (levels - 1) : (piece + 1) * (levels - 1)]:
            copy.wait()
        rows = slice(piece * piece_rows, (piece + 1) * piece_rows)
        total = rel_acc[y, z, rows, :]
        for offset in range(1, levels):
            total = total + z_recv[piece, offset].astype(F32)
        rel_out[rows, :] = total


def hand_over(ent_grad, rel_grad, ent_out, rel_out):
    ent_out[...] = ent_grad[...]
    rel_out[...] = rel_grad[...]


def shards(entities, operators, left_rows, right_rows, negatives, counts):
    buckets = left_rows.shape[0]
    slot_count = left_rows.shape[-1]
    neg_count = negatives.shape[-1]
    groups = lax.axis_size("span")
    doms = lax.axis_size("dom")
    rel_own = operators.shape[0]
    cap = slot_count // (rel_own * groups)
    slots = rel_own * cap
    part_rows, width = entities.shape
    own_rows = part_rows // groups
    out_rows = width // doms
    levels = doms // 2
    chunks = 4 if (rel_own // 4) * out_rows % 16 == 0 else 2
    pieces = 2 if (rel_own // chunks // 2) * out_rows % 16 == 0 else 1
    piece_rows = rel_own // chunks // pieces * out_rows
    half = groups // 2
    mult_rows = part_rows // LANES
    meta_rows = MULT_AT + -(-buckets * mult_rows // 8) * 8
    edges = buckets * groups * cap
    dims = (buckets, doms, groups, rel_own, cap, chunks, pieces)
    dma = pltpu.SemaphoreType.DMA
    vmem = pl.BlockSpec(memory_space=pltpu.VMEM)
    ent_grad, rel_grad = pl.pallas_call(
        functools.partial(kernel, dims),
        out_shape=(
            jax.ShapeDtypeStruct((own_rows, width), F32),
            jax.ShapeDtypeStruct((rel_own * out_rows, width), F32),
        ),
        in_specs=[vmem] * 6,
        out_specs=(vmem, vmem),
        scratch_shapes=[
            pltpu.VMEM((buckets - 1, part_rows, width), BF16),
            pltpu.VMEM((groups, meta_rows, LANES), F32),
            pltpu.VMEM((groups, meta_rows, LANES), F32),
            pltpu.VMEM((rel_own, groups * cap, MULT_AT), F32),
            pltpu.VMEM((buckets, groups * cap, part_rows), F32),
            pltpu.VMEM((buckets, groups * slots, part_rows), BF16),
            pltpu.VMEM((rel_own, edges, width), F32),
            pltpu.VMEM((rel_own, edges, width), F32),
            pltpu.VMEM((rel_own, edges, width), F32),
            pltpu.VMEM((buckets, width, part_rows), F32),
            pltpu.VMEM((buckets, 2, half, own_rows, width), F32),
            pltpu.VMEM((buckets, half, own_rows, width), F32),
            pltpu.VMEM((buckets, half, own_rows, width), BF16),
            pltpu.VMEM((buckets, half, own_rows, width), BF16),
            pltpu.VMEM((buckets, own_rows, width), BF16),
            pltpu.VMEM((buckets, own_rows, width), BF16),
            pltpu.VMEM((2, levels, rel_own * out_rows, width), F32),
            pltpu.VMEM((chunks * pieces, levels, piece_rows, width), BF16),
            pltpu.VMEM((chunks * pieces, levels, piece_rows, width), BF16),
            pltpu.VMEM((chunks * pieces, levels, piece_rows, width), BF16),
            pltpu.VMEM((chunks * pieces, levels, piece_rows, width), BF16),
            dma((groups,)),
            dma((groups,)),
            dma((buckets - 1, groups)),
            dma((buckets - 1, groups)),
            dma((buckets,)),
            dma((buckets,)),
            dma((buckets, half)),
            dma((buckets, half)),
            dma((buckets,)),
            dma((buckets,)),
            dma((chunks * pieces,)),
            dma((chunks * pieces,)),
            dma((chunks * pieces, levels)),
            dma((chunks * pieces, levels)),
        ],
        compiler_params=pltpu.CompilerParams(
            collective_id=0, has_side_effects=True, vmem_limit_bytes=58 * 1024 * 1024
        ),
        name="train_step",
    )(entities, operators, left_rows, right_rows, negatives, counts)
    ent_grad, rel_grad = pl.pallas_call(
        hand_over,
        out_shape=(
            jax.ShapeDtypeStruct(ent_grad.shape, F32),
            jax.ShapeDtypeStruct(rel_grad.shape, F32),
        ),
        in_specs=[vmem] * 2,
        out_specs=(vmem, vmem),
        name="hand_over",
    )(ent_grad, rel_grad)
    return (ent_grad, rel_grad.reshape(rel_own, out_rows, width))


def solution(mesh):
    in_specs = (
        P("dom", None),
        P("span", None, None),
        P(None, "dom", "span", None),
        P(None, "dom", "span", None),
        P(None, "dom", "span", None),
        P(None, "dom", "span", None),
    )
    out_specs = (P(("dom", "span"), None), P("span", "dom", None))
    return jax.shard_map(shards, mesh=mesh, in_specs=in_specs, out_specs=out_specs, check_vma=False)
```
